32 devices in a mesh: dom: 4 (over y, core), narrow: 8 (over z, x).
Axes of the slice: x: 2, y: 2, z: 4, core: 2. Of those that a mesh axis runs over, the one named last changes fastest.
Arguments:
- feats: bfloat16 [32768, 768], P(('dom', 'narrow')), may hold values from -21 to 21
- node_type: int32 [256], P('dom'), may hold values from 0 to 2
- tiles: int32 [256, 4], P('dom'), may hold values from 0 to 63, as said below
- relation: int32 [256, 4], P(('dom', 'narrow')), may hold values from 0 to 4
- neg_sched: int32 [32, 4], P('dom'), may hold values from 0 to 7
- w_query: bfloat16 [3, 768, 768], replicated, may hold values from -0.21875 to 0.21875
- w_key: bfloat16 [3, 768, 768], replicated, may hold values from -0.21875 to 0.21875
- w_value: bfloat16 [3, 768, 768], replicated, may hold values from -0.21875 to 0.21875
- w_out: bfloat16 [3, 768, 768], replicated, may hold values from -0.21875 to 0.21875
- rel_att: bfloat16 [5, 8, 96, 96], replicated, may hold values from -0.625 to 0.625
- rel_msg: bfloat16 [5, 8, 96, 96], replicated, may hold values from -0.625 to 0.625
- rel_prior: float32 [5, 8], replicated, may hold values from 0.5 to 2
- skip_gate: float32 [3], replicated, may hold values from -2 to 2
- pos_view: bfloat16 [32768, 768], P(('dom', 'narrow')), may hold values from -6 to 6
- type_weight: float32 [3], replicated, may hold values from 0.5 to 2
Outputs:
- embedding: bfloat16 [32768, 768], P(('dom', 'narrow'))
- node_loss: float32 [32768], P(('dom', 'narrow'))
- mean_loss: float32 [], replicated
The draws below stay inside these ranges and needn't reach their ends.
Inputs may be any that keep to these rules, and one draw needn't show every extreme that they name: `tiles`: values are block numbers within the target block's group: owner lane times 8 plus the owner's local block. Among the 32 entries of one device's target blocks, at most 5 name blocks of any one lane.
All inputs are finite; a program needn't handle non-finite values.
Results may differ from the reference program's by a relative error of at most 0.008.
The reference program's roundings to bfloat16 on the way (of `attention` and `activated`) count: a program that leaves them out, or rounds other values in their place, can miss the bound.
Values may be sent and summed in bfloat16 or wider, within the bound.
No kernel may reach another device: no remote copies, remote signals or barrier semaphores. Data moves between devices by JAX's collectives and lax.ppermute only.
A program may use at most 128 MiB of HBM per device.

```python
import math
import jax
import jax.numpy as jnp
from jax import lax

D = 768
HEADS = 8
DH = 96
NTYPE = 3
NREL = 5
TILE = 128
NT = 4
TBLK = 8
NODES = 32768
CAP = 5
NEG_STEPS = 4
N_DOM = 4
N_NARROW = 8
DEVICES = 32


def draw_feats(key, part):
    base_key = jax.random.fold_in(jax.random.fold_in(key, 5), 0)
    return jax.random.truncated_normal(base_key, -6.0, 6.0, (NODES, D), jnp.float32).astype(jnp.bfloat16)


def request_owners(device_key):
    hot_key, star_key, base_key, perm_key, tile_key = jax.random.split(device_key, 5)
    slots_all = N_NARROW * CAP
    requests = TBLK * NT
    slot_owner = jnp.arange(slots_all, dtype=jnp.int32) // CAP
    hot_owner = jax.random.randint(hot_key, (2,), 0, N_NARROW)
    star_owner = jax.random.randint(star_key, (), 0, N_NARROW)
    is_hot = jnp.any(slot_owner[:, None] == hot_owner[None, :], axis=1).astype(jnp.int32)
    is_star = (slot_owner == star_owner).astype(jnp.int32)
    scores = jax.random.randint(base_key, (slots_all,), 0, 4096) + 2048 * is_hot + 65536 * is_star
    ranked = jnp.argsort(-(scores * slots_all + jnp.arange(slots_all, dtype=jnp.int32)))
    owners = slot_owner[ranked[:requests]]
    owners = owners[jax.random.permutation(perm_key, requests)]
    local_block = jax.random.randint(tile_key, (requests,), 0, TBLK)
    return (owners * TBLK + local_block).reshape(TBLK, NT)


def draw_tiles(key, part):
    device_keys = jax.random.split(jax.random.fold_in(key, 17), N_DOM * N_NARROW)
    per_device = jax.vmap(request_owners)(device_keys)
    return per_device.reshape(N_DOM * N_NARROW * TBLK, NT).astype(jnp.int32)


def with_ends(result, own_key, low, high):
    shape = result.shape
    index_at = [jax.random.randint(jax.random.fold_in(own_key, axis), (), 0, shape[axis]) for axis in range(len(shape))]
    result = result.at[tuple(index_at)].set(low)
    longest = shape.index(max(shape))
    index_at[longest] = (index_at[longest] + 1) % shape[longest]
    return result.at[tuple(index_at)].set(high)


def levels(own_key, dims, cuts, least, high):
    gain = 1.0
    for position, blocks in cuts:
        heights = jax.random.uniform(jax.random.fold_in(jax.random.fold_in(own_key, 6), position), (blocks,), jnp.float32, least / len(cuts), high / len(cuts))
        gain = gain * jnp.repeat(jnp.exp(heights), dims[position] // blocks).reshape((-1,) + (1,) * (len(dims) - 1 - position))
    return gain


def gaussian(stream_key, shape, deviation, limit, pieces=(), held_as=jnp.bfloat16):
    gain = levels(stream_key, shape, pieces, -0.22, 0.18) if pieces else 1.0
    drawn = jax.random.normal(stream_key, shape, jnp.float32) * deviation * gain
    return jnp.minimum(jnp.maximum(drawn, -limit), limit).astype(held_as)


def setup_inputs(seed: int = 0) -> dict:
    seeds = jax.random.split(jax.random.key(seed), 16)
    feats = draw_feats(jax.random.fold_in(seeds[15], 71), 0)
    node_type = with_ends(jax.random.randint(seeds[1], (NODES // TILE,), 0, NTYPE), jax.random.fold_in(seeds[1], 1), 0, NTYPE - 1).astype(jnp.int32)
    tiles = draw_tiles(jax.random.fold_in(seeds[15], 71), 0)
    relation = with_ends(jax.random.randint(seeds[3], (NODES // TILE, NT), 0, NREL), jax.random.fold_in(seeds[3], 1), 0, NREL - 1).astype(jnp.int32)
    neg_sched = with_ends(jax.random.randint(seeds[4], (DEVICES, NEG_STEPS), 0, TBLK), jax.random.fold_in(seeds[4], 1), 0, TBLK - 1).astype(jnp.int32)
    w_query = gaussian(seeds[5], (NTYPE, D, D), D ** -0.5, 0.21875)
    w_key = gaussian(seeds[6], (NTYPE, D, D), D ** -0.5, 0.21875)
    w_value = gaussian(seeds[7], (NTYPE, D, D), D ** -0.5, 0.21875)
    w_out = gaussian(seeds[8], (NTYPE, D, D), D ** -0.5, 0.21875)
    rel_att = gaussian(seeds[9], (NREL, HEADS, DH, DH), DH ** -0.5, 0.625)
    rel_msg = gaussian(seeds[10], (NREL, HEADS, DH, DH), DH ** -0.5, 0.625)
    rel_prior = jnp.clip(jnp.exp(jax.random.uniform(seeds[11], (NREL, HEADS), jnp.float32, math.log(0.5), math.log(2.0))), 0.5, 2.0)
    skip_gate = jnp.clip(jax.random.uniform(seeds[12], (NTYPE,), jnp.float32, -2.0, 2.0), -2.0, 2.0)
    pos_view = gaussian(seeds[13], (NODES, D), 1.0, 6.0, ((0, 32),))
    type_weight = jnp.clip(jnp.exp(jax.random.uniform(seeds[14], (NTYPE,), jnp.float32, math.log(0.5), math.log(2.0))), 0.5, 2.0)
    return {"feats": feats, "node_type": node_type, "tiles": tiles, "relation": relation, "neg_sched": neg_sched, "w_query": w_query, "w_key": w_key, "w_value": w_value, "w_out": w_out, "rel_att": rel_att, "rel_msg": rel_msg, "rel_prior": rel_prior, "skip_gate": skip_gate, "pos_view": pos_view, "type_weight": type_weight}


def rounded(values):
    return lax.optimization_barrier(values.astype(jnp.bfloat16))

def reference(feats, node_type, tiles, relation, neg_sched, w_query, w_key, w_value, w_out, rel_att, rel_msg, rel_prior, skip_gate, pos_view, type_weight):
    nblocks = NODES // TILE
    blocks = feats.reshape(nblocks, TILE, D)

    def project(inputs):
        block_rows, type_id = inputs
        return tuple((rounded(jnp.dot(block_rows, weight[type_id], preferred_element_type=jnp.float32)) for weight in (w_query, w_key, w_value)))
    queries, keys_all, values_all = lax.map(project, (blocks, node_type))
    group_size = N_NARROW * TBLK
    block_ids = jnp.arange(nblocks, dtype=jnp.int32)
    sources = tiles + (block_ids // group_size * group_size)[:, None]

    def attend(inputs):
        query_block, own_rows, source_ids, rel_ids, type_id = inputs
        src_keys = keys_all[source_ids].reshape(NT, TILE, HEADS, DH).astype(jnp.float32)
        src_values = values_all[source_ids].reshape(NT, TILE, HEADS, DH).astype(jnp.float32)
        keyed_rows = rounded(jnp.einsum('jmhd,jhde->jmhe', src_keys, rel_att[rel_ids].astype(jnp.float32), precision=lax.Precision.HIGHEST))
        message = rounded(jnp.einsum('jmhd,jhde->jmhe', src_values, rel_msg[rel_ids].astype(jnp.float32), precision=lax.Precision.HIGHEST))
        heads_query = query_block.reshape(TILE, HEADS, DH).astype(jnp.float32)
        scores = jnp.einsum('ihd,jmhd->hijm', heads_query, keyed_rows.astype(jnp.float32), precision=lax.Precision.HIGHEST)
        prior_scale = jnp.transpose(rel_prior[rel_ids]) / math.sqrt(DH)
        scores = (scores * prior_scale[:, None, :, None]).reshape(HEADS, TILE, NT * TILE)
        highest = lax.optimization_barrier(jnp.max(scores, axis=2, keepdims=True))
        exponent = jnp.exp(scores - highest)
        attention = rounded(exponent / lax.optimization_barrier(jnp.sum(exponent, axis=2, keepdims=True)))
        merged = jnp.einsum('hin,nhe->ihe', attention.astype(jnp.float32), message.reshape(NT * TILE, HEADS, DH).astype(jnp.float32), precision=lax.Precision.HIGHEST)
        activated = jax.nn.gelu(merged.reshape(TILE, D), approximate=False).astype(jnp.bfloat16)
        projected = jnp.dot(activated, w_out[type_id], preferred_element_type=jnp.float32)
        mix_gate = jax.nn.sigmoid(skip_gate[type_id])
        return (mix_gate * projected + (1.0 - mix_gate) * own_rows.astype(jnp.float32)).astype(jnp.bfloat16)
    out_blocks = lax.map(attend, (queries, blocks, sources, relation, node_type))
    device_of = block_ids // TBLK
    group_of = device_of // N_NARROW
    lane_of = device_of % N_NARROW
    offsets = jnp.arange(1, NEG_STEPS + 1, dtype=jnp.int32)
    sender = group_of[:, None] * N_NARROW + (lane_of[:, None] - offsets[None, :]) % N_NARROW
    neg_ids = (sender * TBLK + neg_sched[sender, offsets[None, :] - 1]).astype(jnp.int32)

    def contrast(inputs):
        own_out, own_pos, neg_block_ids, type_id = inputs
        own_float = own_out.astype(jnp.float32)
        positive = lax.optimization_barrier(jnp.sum(own_float * own_pos.astype(jnp.float32), axis=1)) / math.sqrt(D)
        neg_rows = out_blocks[neg_block_ids].reshape(NEG_STEPS * TILE, D).astype(jnp.float32)
        neg_logits = jnp.einsum('nd,md->nm', own_float, neg_rows, precision=lax.Precision.HIGHEST) / math.sqrt(D)
        same_type = jnp.repeat(node_type[neg_block_ids] == type_id, TILE, total_repeat_length=NEG_STEPS * TILE)
        neg_logits = jnp.where(same_type[None, :], neg_logits, -jnp.inf)
        highest = jnp.maximum(positive, lax.optimization_barrier(jnp.max(neg_logits, axis=1)))
        denominator = jnp.exp(positive - highest) + lax.optimization_barrier(jnp.sum(jnp.exp(neg_logits - highest[:, None]), axis=1))
        return highest + jnp.log(denominator) - positive
    node_loss = lax.map(contrast, (out_blocks, pos_view.reshape(nblocks, TILE, D), neg_ids, node_type)).reshape(NODES)
    row_weight = jnp.repeat(type_weight[node_type], TILE, total_repeat_length=NODES)
    mean_loss = jnp.sum(row_weight * node_loss) / NODES
    return (out_blocks.reshape(NODES, D), node_loss, mean_loss)
```

```python
import functools
import math

import jax
import jax.numpy as jnp
from jax import lax
from jax.experimental import pallas as pl
from jax.experimental.pallas import tpu as pltpu
from jax.sharding import PartitionSpec as P

TILE = 128
LANES = 128
MXU = 256
F32 = jnp.float32
BF16 = jnp.bfloat16
VMEM_LIMIT = 48 * 1024 * 1024

OWN, PARTNER, BELOW, ABOVE, BELOW_X, ABOVE_X, FAR_UP, FAR_DOWN, FAR_X, ENDS, ENDS_X = range(11)
PHASES = 4


def params(cost=None):
    return dict(
        compiler_params=pltpu.CompilerParams(vmem_limit_bytes=VMEM_LIMIT),
        cost_estimate=cost,
    )


def cost(flops, nbytes, trans=0):
    return pl.CostEstimate(flops=int(flops), bytes_accessed=int(nbytes), transcendentals=int(trans))


class Layout:
    def __init__(self, lanes, nblocks, slots, steps, types):
        self.lanes, self.nblocks, self.slots, self.steps, self.types = (
            lanes, nblocks, slots, steps, types,
        )
        self.requests = nblocks * slots
        self.cap = (self.requests + lanes - 1) // lanes + 1
        at = 0
        for name, size in (
            ("partner", lanes * self.cap),
            ("ends", lanes * self.cap),
            ("ends_x", lanes * self.cap),
            ("start", PHASES + 1),
            ("slot", self.requests),
            ("buf", self.requests),
            ("idx", self.requests),
            ("kind", self.requests),
            ("rel", self.requests),
            ("qblk", nblocks),
            ("qkind", nblocks),
            ("own_kind", nblocks),
            ("offer", nblocks),
            ("sched", steps),
            ("neg_kind", steps),
            ("lane", 1),
        ):
            setattr(self, name, at)
            at += size
        self.size = at


def plan_body(lay, staged, lane_ref, tiles, kinds, relation, sched, out, count, keys, bufs, idxs):
    lanes, nblocks, slots, steps, types = lay.lanes, lay.nblocks, lay.slots, lay.steps, lay.types
    cap, requests = lay.cap, lay.requests
    lane = lane_ref[0]
    depth, side = lane // 2, lax.rem(lane, 2)

    def clear(ref, base, size):
        def one(i, _):
            ref[base + i] = 0
            return 0

        lax.fori_loop(0, size, one, 0)

    def lists_of(device, base):
        clear(count, 0, lanes)
        clear(out, base, lanes * cap)

        def one(i, _):
            tile = tiles[device * nblocks + i // slots, lax.rem(i, slots)]
            owner = tile // nblocks
            rank = count[owner]
            out[base + owner * cap + rank] = lax.rem(tile, nblocks)
            count[owner] = rank + 1
            return 0

        lax.fori_loop(0, requests, one, 0)

    out[lay.lane] = lane
    if staged:
        far = lanes // 2 - 1 - depth
        lists_of(lane + 1 - 2 * side, lay.partner)
        lists_of(far * 2 + side, lay.ends)
        lists_of(far * 2 + 1 - side, lay.ends_x)

    clear(count, 0, lanes)
    clear(keys, 0, PHASES * types)

    def place(i, _):
        tile = tiles[lane * nblocks + i // slots, lax.rem(i, slots)]
        kind = kinds[tile]
        if staged:
            owner, local = tile // nblocks, lax.rem(tile, nblocks)
            rank = count[owner]
            count[owner] = rank + 1
            delta = owner // 2 - depth
            same = lax.rem(owner, 2) == side
            away = jnp.abs(delta)
            near = jnp.where(
                same,
                jnp.where(delta > 0, ABOVE, BELOW),
                jnp.where(delta > 0, ABOVE_X, BELOW_X),
            )
            buf = jnp.where(
                away == 0,
                jnp.where(same, OWN, PARTNER),
                jnp.where(
                    away == 1,
                    near,
                    jnp.where(
                        away == 2,
                        jnp.where(same, jnp.where(delta > 0, FAR_DOWN, FAR_UP), FAR_X),
                        jnp.where(same, ENDS, ENDS_X),
                    ),
                ),
            )
            whole = jnp.logical_and(same, away <= 2)
            idx = jnp.where(whole, local, rank)
            late = jnp.where(
                away == 0,
                0,
                jnp.where(
                    away == 1,
                    jnp.where(same, 0, 1),
                    jnp.where(away == 2, jnp.where(same, 1, 2), 3),
                ),
            )
        else:
            buf, idx, late = jnp.int32(OWN), tile, jnp.int32(0)
        key = late * types + kind
        bufs[i] = buf
        idxs[i] = idx
        bufs[requests + i] = key
        bufs[2 * requests + i] = kind
        keys[key] = keys[key] + 1
        return 0

    lax.fori_loop(0, requests, place, 0)

    total = jnp.int32(0)
    for phase in range(PHASES):
        out[lay.start + phase] = total
        for kind in range(types):
            key = phase * types + kind
            size = keys[key]
            keys[key] = total
            total = total + size
    out[lay.start + PHASES] = total

    def order(i, _):
        key = bufs[requests + i]
        at = keys[key]
        keys[key] = at + 1
        out[lay.slot + at] = i
        out[lay.buf + at] = bufs[i]
        out[lay.idx + at] = idxs[i]
        out[lay.kind + at] = bufs[2 * requests + i]
        out[lay.rel + at] = relation[i // slots, lax.rem(i, slots)]
        return 0

    lax.fori_loop(0, requests, order, 0)

    at = jnp.int32(0)
    for kind in range(types):
        for block in range(nblocks):
            mine = kinds[lane * nblocks + block]
            hit = mine == kind

            @pl.when(hit)
            def _(at=at, block=block, kind=kind):
                out[lay.qblk + at] = block
                out[lay.qkind + at] = kind

            at = at + hit.astype(jnp.int32)
    for block in range(nblocks):
        out[lay.own_kind + block] = kinds[lane * nblocks + block]
        out[lay.offer + block] = -1
    for step in range(steps):
        block = sched[lane, step]
        out[lay.sched + step] = block
        out[lay.offer + block] = step
        sender = lax.rem(lane - (step + 1) + lanes, lanes)
        out[lay.neg_kind + step] = kinds[sender * nblocks + sched[sender, step]]


def make_plan(lay, staged, lane, tiles, kinds, relation, sched):
    smem = pl.BlockSpec(memory_space=pltpu.SMEM)
    return pl.pallas_call(
        functools.partial(plan_body, lay, staged),
        out_shape=jax.ShapeDtypeStruct((lay.size,), jnp.int32),
        in_specs=[smem] * 5,
        out_specs=smem,
        scratch_shapes=[
            pltpu.SMEM((lay.lanes,), jnp.int32),
            pltpu.SMEM((PHASES * lay.types,), jnp.int32),
            pltpu.SMEM((3 * lay.requests,), jnp.int32),
            pltpu.SMEM((lay.requests,), jnp.int32),
        ],
        cost_estimate=cost(1e5, 4096),
        name="plan",
    )(lane, tiles, kinds, relation, sched)


class Heads:
    def __init__(self, heads, size, width):
        self.heads, self.size, self.width = heads, size, width
        self.padded = heads * LANES
        self.pieces = []
        self.spots = []
        row = 0
        for pair in range(heads // 2):
            first = pair * 2 * size
            low = first // MXU * MXU
            high = min(-(-(first + 2 * size) // MXU) * MXU, width)
            self.pieces.append((row, low, high - low, pair * 2 * LANES))
            for half in range(2):
                self.spots.append((row + first + half * size - low, half * LANES))
            row += high - low
        self.rows = row

    def apply(self, rows, matrix, out):
        for at, low, columns, to in self.pieces:
            out[0, :, to : to + 2 * LANES] = jnp.dot(
                rows[:, low : low + columns],
                matrix[0, at : at + columns, :],
                preferred_element_type=F32,
            ).astype(BF16)


def spread_body(hd, att, msg, out_att, out_msg):
    last = pl.program_id(0) == pl.num_programs(0) - 1
    rows = lax.broadcasted_iota(jnp.int32, (hd.size, hd.size), 0)
    columns = lax.broadcasted_iota(jnp.int32, (hd.size, hd.size), 1)
    eye = (rows == columns).astype(BF16)
    for src, out in ((att, out_att), (msg, out_msg)):
        out[...] = jnp.zeros_like(out)
        for head, (row, column) in enumerate(hd.spots):
            out[0, row : row + hd.size, column : column + hd.size] = jnp.where(
                last, eye, src[0, head]
            )


def spread(hd, att, msg):
    count = att.shape[0]
    source = pl.BlockSpec(
        (1,) + att.shape[1:], lambda i: (jnp.minimum(i, count - 1), 0, 0, 0)
    )
    target = pl.BlockSpec((1, hd.rows, 2 * LANES), lambda i: (i, 0, 0))
    shape = jax.ShapeDtypeStruct((count + 1, hd.rows, 2 * LANES), BF16)
    return pl.pallas_call(
        functools.partial(spread_body, hd),
        grid=(count + 1,),
        in_specs=[source, source],
        out_specs=[target, target],
        out_shape=[shape, shape],
        name="spread",
        **params(cost(1e6, 4 * (count + 1) * hd.rows * 2 * LANES)),
    )(att, msg)


def query_body(lay, hd, plan, rows, weight, pieces, out):
    held = jnp.dot(rows[0], weight[0], preferred_element_type=F32).astype(BF16)
    hd.apply(held, pieces, out)


def queries(lay, hd, plan, blocks, weight, pieces):
    width = blocks.shape[2]
    identity = pieces.shape[0] - 1
    return pl.pallas_call(
        functools.partial(query_body, lay, hd),
        grid_spec=pltpu.PrefetchScalarGridSpec(
            num_scalar_prefetch=1,
            grid=(lay.nblocks,),
            in_specs=[
                pl.BlockSpec((1, TILE, width), lambda i, plan: (plan[lay.qblk + i], 0, 0)),
                pl.BlockSpec((1, width, width), lambda i, plan: (plan[lay.qkind + i], 0, 0)),
                pl.BlockSpec((1, hd.rows, 2 * LANES), lambda i, plan: (identity, 0, 0)),
            ],
            out_specs=pl.BlockSpec(
                (1, TILE, hd.padded), lambda i, plan: (plan[lay.qblk + i], 0, 0)
            ),
        ),
        out_shape=jax.ShapeDtypeStruct((lay.nblocks, TILE, hd.padded), BF16),
        name="queries",
        **params(cost(2e9, 10e6)),
    )(plan, blocks, weight, pieces)


def pick_body(wanted, nbufs, plan, *refs):
    sources, outs, sem = refs[:nbufs], refs[nbufs:-1], refs[-1]
    copies = []
    for out, (choose, cap) in zip(outs, wanted):
        for k in range(cap):
            copies.append(choose(plan, sources, out.at[k], k, sem.at[len(copies)]))
    for wait in copies:
        wait()


def pick(lay, plan, sources, wanted):
    def chooser(base_of, source_of):
        def choose(plan_ref, refs, target, k, sem):
            block = plan_ref[base_of(plan_ref) + k]
            source_of(plan_ref, refs, block, target, sem)
            return lambda: pltpu.make_async_copy(refs[0].at[0], target, sem).wait()

        return choose

    shape = sources[0].shape[1:]
    anywhere = pl.BlockSpec(memory_space=pl.ANY)
    count = len(wanted) * lay.cap
    return pl.pallas_call(
        functools.partial(
            pick_body, [(chooser(b, s), lay.cap) for b, s in wanted], len(sources)
        ),
        grid_spec=pltpu.PrefetchScalarGridSpec(
            num_scalar_prefetch=1,
            grid=(),
            in_specs=[anywhere] * len(sources),
            out_specs=[anywhere] * len(wanted),
            scratch_shapes=[pltpu.SemaphoreType.DMA((count,))],
        ),
        out_shape=[jax.ShapeDtypeStruct((lay.cap,) + shape, BF16)] * len(wanted),
        name="pick",
        **params(cost(1e3, count * 4 * shape[0] * shape[1])),
    )(plan, *sources)


def source_body(lay, hd, phase, codes, plan, *refs):
    nbufs = len(codes)
    bufs = refs[:nbufs]
    w_key, w_value, p_att, p_msg = refs[nbufs : nbufs + 4]
    keyed, message, held, sem = refs[-4:]
    step = pl.program_id(0)
    start = plan[lay.start + phase]
    count = plan[lay.start + phase + 1] - start

    def fetch(at):
        into = lax.rem(at, 2)
        which, block = plan[lay.buf + start + at], plan[lay.idx + start + at]
        for code, ref in zip(codes, bufs):

            @pl.when(which == code)
            def _(ref=ref):
                pltpu.make_async_copy(ref.at[block], held.at[into], sem.at[into]).start()

    @pl.when(jnp.logical_and(step == 0, count > 0))
    def _():
        fetch(0)

    @pl.when(step + 1 < count)
    def _():
        fetch(step + 1)

    @pl.when(step < count)
    def _():
        now = lax.rem(step, 2)
        pltpu.make_async_copy(bufs[0].at[0], held.at[now], sem.at[now]).wait()
        rows = held[now]
        key = jnp.dot(rows, w_key[0], preferred_element_type=F32).astype(BF16)
        hd.apply(key, p_att, keyed)
        value = jnp.dot(rows, w_value[0], preferred_element_type=F32).astype(BF16)
        hd.apply(value, p_msg, message)


def sources_of(lay, hd, plan, phase, most, bufs, w_key, w_value, p_att, p_msg, before):
    codes = list(bufs)
    width = w_key.shape[1]
    spare = lay.requests

    def last(i, plan):
        start = plan[lay.start + phase]
        count = plan[lay.start + phase + 1] - start
        return jnp.minimum(start + jnp.minimum(i, jnp.maximum(count - 1, 0)), lay.requests - 1)

    def kind(i, plan):
        return plan[lay.kind + last(i, plan)], 0, 0

    def rel(i, plan):
        return plan[lay.rel + last(i, plan)], 0, 0

    def slot(i, plan):
        count = plan[lay.start + phase + 1] - plan[lay.start + phase]
        return jnp.where(i < count, plan[lay.slot + last(i, plan)], spare), 0, 0

    anywhere = pl.BlockSpec(memory_space=pl.ANY)
    weight = pl.BlockSpec((1, width, width), kind)
    piece = pl.BlockSpec((1, hd.rows, 2 * LANES), rel)
    target = pl.BlockSpec((1, TILE, hd.padded), slot)
    shape = jax.ShapeDtypeStruct((spare + lay.slots, TILE, hd.padded), BF16)
    first = 1 + len(codes) + 4
    flops = most * 2 * TILE * 2 * (width * width + hd.rows * 2 * LANES)
    return pl.pallas_call(
        functools.partial(source_body, lay, hd, phase, codes),
        grid_spec=pltpu.PrefetchScalarGridSpec(
            num_scalar_prefetch=1,
            grid=(most,),
            in_specs=[anywhere] * len(codes)
            + [weight, weight, piece, piece]
            + [anywhere] * len(before),
            out_specs=[target, target],
            scratch_shapes=[
                pltpu.VMEM((2, TILE, width), BF16),
                pltpu.SemaphoreType.DMA((2,)),
            ],
        ),
        out_shape=[shape, shape],
        input_output_aliases={first + k: k for k in range(len(before))},
        name="sources",
        **params(cost(flops, most * 2.4e6)),
    )(plan, *bufs.values(), w_key, w_value, p_att, p_msg, *before)


def finish(hd, slots, priors, query, keyed, message, w_out, own, mix, put):
    heads = []
    for head in range(hd.heads):
        at = slice(head * LANES, (head + 1) * LANES)
        q = query[0, :, at]
        scores = []
        for slot in range(slots):
            score = lax.dot_general(
                q, keyed[slot, :, at], (((1,), (1,)), ((), ())), preferred_element_type=F32
            )
            scores.append(score * priors(slot, head))
        scores = jnp.concatenate(scores, axis=1)
        highest = jnp.max(scores, axis=1, keepdims=True)
        exponent = jnp.exp(scores - highest)
        share = 1.0 / jnp.sum(exponent, axis=1, keepdims=True)
        attention = (exponent * share).astype(BF16)
        merged = jnp.dot(
            attention,
            message[:, :, at].reshape(slots * TILE, LANES),
            preferred_element_type=F32,
        )
        active = 0.5 * merged * (1.0 + lax.erf(merged * math.sqrt(0.5)))
        heads.append(active.astype(BF16))
    projected = jnp.dot(
        jnp.concatenate(heads, axis=1), w_out[0], preferred_element_type=F32
    )
    put((mix * projected + (1.0 - mix) * own[0].astype(F32)).astype(BF16))


def prior_of(lay, relation, prior, block, hd):
    def priors(slot, head):
        return prior[relation[block, slot], head] * (1.0 / math.sqrt(hd.size))

    return priors


def offers_body(lay, hd, plan, relation, prior, mix, query, keyed, message, w_out, own, *outs):
    step = pl.program_id(0)
    block = plan[lay.sched + step]

    def put(rows):
        for k, out in enumerate(outs):

            @pl.when(step == k)
            def _(out=out):
                out[...] = rows

    finish(
        hd, lay.slots, prior_of(lay, relation, prior, block, hd), query, keyed, message,
        w_out, own, mix[plan[lay.own_kind + block]], put,
    )


def rest_body(lay, hd, plan, relation, prior, mix, query, keyed, message, w_out, own, *refs):
    offers, out = refs[:-1], refs[-1]
    block = pl.program_id(0)
    offered = plan[lay.offer + block]
    for k, ref in enumerate(offers):

        @pl.when(offered == k)
        def _(ref=ref):
            out[0] = ref[...]

    @pl.when(offered < 0)
    def _():
        def put(rows):
            out[0] = rows

        finish(
            hd, lay.slots, prior_of(lay, relation, prior, block, hd), query, keyed, message,
            w_out, own, mix[plan[lay.own_kind + block]], put,
        )


def attend(lay, hd, plan, relation, prior, mix, query, keyed, message, w_out, blocks, offers):
    width = blocks.shape[2]
    first = offers is None
    smem = pl.BlockSpec(memory_space=pltpu.SMEM)

    def block_at(i, plan):
        return plan[lay.sched + i] if first else i

    def at(i, plan):
        return block_at(i, plan), 0, 0

    def kind(i, plan):
        return plan[lay.own_kind + block_at(i, plan)], 0, 0

    in_specs = [
        smem, smem, smem,
        pl.BlockSpec((1, TILE, hd.padded), at),
        pl.BlockSpec((lay.slots, TILE, hd.padded), at),
        pl.BlockSpec((lay.slots, TILE, hd.padded), at),
        pl.BlockSpec((1, hd.padded, width), kind),
        pl.BlockSpec((1, TILE, width), at),
    ]
    whole = pl.BlockSpec((TILE, width), lambda i, plan: (0, 0))
    one = jax.ShapeDtypeStruct((TILE, width), BF16)
    count = lay.steps if first else lay.nblocks
    work = cost(count * 5e8, count * 3e6, count * hd.heads * lay.slots * TILE * TILE)
    args = (plan, relation, prior, mix, query, keyed, message, w_out, blocks)
    return pl.pallas_call(
        functools.partial(offers_body if first else rest_body, lay, hd),
        grid_spec=pltpu.PrefetchScalarGridSpec(
            num_scalar_prefetch=1,
            grid=(count,),
            in_specs=in_specs if first else in_specs + [whole] * lay.steps,
            out_specs=[whole] * lay.steps if first else pl.BlockSpec((1, TILE, width), at),
        ),
        out_shape=[one] * lay.steps
        if first
        else jax.ShapeDtypeStruct((lay.nblocks, TILE, width), BF16),
        name="offers" if first else "rest",
        **params(work),
    )(*args, *(() if first else offers))


def contrast_body(lay, scale, plan, weights, rows, views, *refs):
    negs, loss, total = refs[: lay.steps], refs[-2], refs[-1]
    block = pl.program_id(0)
    kind = plan[lay.own_kind + block]
    mine = rows[0]
    product = mine.astype(F32) * views[0].astype(F32)
    width = product.shape[1]
    folded = product[:, :LANES]
    for at in range(LANES, width, LANES):
        folded = folded + product[:, at : at + LANES]
    positive = jnp.sum(folded.T, axis=0, keepdims=True) * scale
    logits = []
    for step in range(lay.steps):
        logit = lax.dot_general(
            negs[step][...], mine, (((1,), (1,)), ((), ())), preferred_element_type=F32
        )
        match = plan[lay.neg_kind + step] == kind
        logits.append(jnp.where(match, logit * scale, -jnp.inf))
    highest = positive
    for logit in logits:
        highest = jnp.maximum(highest, jnp.max(logit, axis=0, keepdims=True))
    denominator = jnp.exp(positive - highest)
    for logit in logits:
        denominator = denominator + jnp.sum(jnp.exp(logit - highest), axis=0, keepdims=True)
    result = highest + jnp.log(denominator) - positive
    loss[pl.ds(block, 1), :] = result

    @pl.when(block == 0)
    def _():
        total[...] = jnp.zeros_like(total)

    total[...] += jnp.sum(result, axis=1, keepdims=True) * weights[kind]


def contrast(lay, plan, weights, rows, views, negs):
    width = rows.shape[2]
    at = pl.BlockSpec((1, TILE, width), lambda i, plan: (i, 0, 0))
    whole = pl.BlockSpec((TILE, width), lambda i, plan: (0, 0))
    return pl.pallas_call(
        functools.partial(contrast_body, lay, 1.0 / math.sqrt(width)),
        grid_spec=pltpu.PrefetchScalarGridSpec(
            num_scalar_prefetch=1,
            grid=(lay.nblocks,),
            in_specs=[pl.BlockSpec(memory_space=pltpu.SMEM), at, at] + [whole] * lay.steps,
            out_specs=[
                pl.BlockSpec((lay.nblocks, TILE), lambda i, plan: (0, 0)),
                pl.BlockSpec((1, 1), lambda i, plan: (0, 0)),
            ],
        ),
        out_shape=[
            jax.ShapeDtypeStruct((lay.nblocks, TILE), F32),
            jax.ShapeDtypeStruct((1, 1), F32),
        ],
        name="contrast",
        **params(cost(1e9, 4e6, 5e5)),
    )(plan, weights, rows, views, *negs)


def summed(value, axis):
    count = lax.axis_size(axis)
    if count & (count - 1):
        return lax.psum(value, axis)
    bit = 1
    while bit < count:
        value = value + lax.ppermute(value, axis, [(i, i ^ bit) for i in range(count)])
        bit *= 2
    return value


def shards(
    feats,
    node_type,
    tiles,
    relation,
    neg_sched,
    w_query,
    w_key,
    w_value,
    w_out,
    rel_att,
    rel_msg,
    rel_prior,
    skip_gate,
    pos_view,
    type_weight,
):
    lanes = lax.axis_size("narrow")
    lane = lax.axis_index("narrow")
    width = feats.shape[1]
    nblocks = feats.shape[0] // TILE
    heads, size = rel_att.shape[1], rel_att.shape[2]
    lay = Layout(lanes, nblocks, tiles.shape[1], neg_sched.shape[1], w_query.shape[0])
    hd = Heads(heads, size, width)
    staged = lanes == 8
    blocks = feats.reshape(nblocks, TILE, width)
    cap = lay.cap

    plan = make_plan(
        lay, staged, lane.astype(jnp.int32).reshape(1), tiles, node_type, relation, neg_sched
    )
    p_att, p_msg = spread(hd, rel_att, rel_msg)
    padded_out = jnp.pad(
        w_out.reshape(-1, heads, size, width), ((0, 0), (0, 0), (0, LANES - size), (0, 0))
    ).reshape(-1, hd.padded, width)
    mix = jax.nn.sigmoid(skip_gate)
    query = queries(lay, hd, plan, blocks, w_query, p_att)

    def project(phase, most, bufs, before):
        return sources_of(
            lay, hd, plan, phase, most, bufs, w_key, w_value, p_att, p_msg, before
        )

    if staged:
        deep = lanes // 2

        def moved(array, pairs):
            return lax.ppermute(array, "narrow", pairs)

        ups = [(2 * z + x, 2 * z + 2 + x) for z in range(deep - 1) for x in range(2)]
        downs = [(b, a) for a, b in ups]

        def swaps(depths):
            return [(2 * z + x, 2 * z + 1 - x) for z in depths for x in range(2)]

        def from_first(plan, refs, block, target, sem):
            pltpu.make_async_copy(refs[0].at[block], target, sem).start()

        def from_second(plan, refs, block, target, sem):
            pltpu.make_async_copy(refs[1].at[block], target, sem).start()

        def from_far(plan, refs, block, target, sem):
            low = plan[lay.lane] // 2 < deep // 2

            @pl.when(low)
            def _():
                pltpu.make_async_copy(refs[1].at[block], target, sem).start()

            @pl.when(jnp.logical_not(low))
            def _():
                pltpu.make_async_copy(refs[0].at[block], target, sem).start()

        def own_list(base):
            return lambda plan: base + plan[lay.lane] * cap

        def list_at(offset):
            def base_of(plan):
                other = plan[lay.lane] + 2 * offset
                return lay.partner + jnp.clip(other, 0, lanes - 1) * cap

            return base_of

        def far_list(plan):
            mine = plan[lay.lane]
            return lay.partner + jnp.where(mine // 2 < deep // 2, mine + 4, mine - 4) * cap

        below = moved(blocks, ups)
        above = moved(blocks, downs)
        out_partner, out_ends, out_ends_x = pick(
            lay, plan, [blocks],
            [
                (own_list(lay.partner), from_first),
                (own_list(lay.ends), from_first),
                (own_list(lay.ends_x), from_first),
            ],
        )
        partner = moved(out_partner, swaps(range(deep)))
        relay = moved(out_ends_x, swaps((0, deep - 1)))

        far_below = moved(below, [p for p in ups if 2 <= p[0] < lanes - 2])
        far_above = moved(above, [p for p in downs if 2 <= p[0] < lanes - 2])
        out_below, out_above = pick(
            lay, plan, [below, above],
            [(list_at(-1), from_first), (list_at(1), from_second)],
        )
        below_x = moved(out_below, swaps(range(1, deep)))
        above_x = moved(out_above, swaps(range(deep - 1)))

        (out_far,) = pick(lay, plan, [far_below, far_above], [(far_list, from_far)])
        far_x = moved(out_far, swaps(range(deep)))
        out_ends, relay, far_below, far_above = lax.optimization_barrier(
            (out_ends, relay, far_below, far_above)
        )
        last = lanes - 2
        corners = [(x, last + x) for x in range(2)] + [(last + x, x) for x in range(2)]
        ends = moved(out_ends, corners)
        ends_x = moved(relay, corners)

        made = project(
            0, min(2 * cap + 2 * cap, lay.requests),
            {OWN: blocks, PARTNER: partner, BELOW: below, ABOVE: above}, (),
        )
        made = project(
            1, min(3 * cap, lay.requests),
            {BELOW_X: below_x, ABOVE_X: above_x, FAR_UP: far_below, FAR_DOWN: far_above}, made,
        )
        made = project(2, cap, {FAR_X: far_x}, made)
        made = project(3, min(2 * cap, lay.requests), {ENDS: ends, ENDS_X: ends_x}, made)
    else:
        gathered = lax.all_gather(blocks, "narrow", tiled=True)
        made = project(0, lay.requests, {OWN: gathered}, ())

    keyed, message = made
    shared = (lay, hd, plan, relation, rel_prior, mix, query, keyed, message, padded_out, blocks)
    offers = attend(*shared, None)
    negs = [
        lax.ppermute(
            offers[step], "narrow", [(i, (i + step + 1) % lanes) for i in range(lanes)]
        )
        for step in range(lay.steps)
    ]
    embedding = attend(*shared, offers)
    node_loss, total = contrast(
        lay, plan, type_weight, embedding, pos_view.reshape(nblocks, TILE, width), negs
    )
    total = summed(summed(total, "dom"), "narrow")
    nodes = node_loss.size * lax.axis_size("dom") * lanes
    return (
        embedding.reshape(nblocks * TILE, width),
        node_loss.reshape(nblocks * TILE),
        total[0, 0] / nodes,
    )


def solution(mesh):
    return jax.shard_map(
        shards,
        mesh=mesh,
        in_specs=(
            P(("dom", "narrow"), None),
            P("dom"),
            P("dom", None),
            P(("dom", "narrow"), None),
            P("dom", None),
            P(),
            P(),
            P(),
            P(),
            P(),
            P(),
            P(),
            P(),
            P(("dom", "narrow"), None),
            P(),
        ),
        out_specs=(P(("dom", "narrow"), None), P(("dom", "narrow")), P()),
        check_vma=False,
    )
```
